256 devices in a mesh: row: 16 (over z, core), col: 16 (over x, y).
Axes of the slice: x: 4, y: 4, z: 8, core: 2. Of those that a mesh axis runs over, the one named last changes fastest.
Arguments:
- matrix: bfloat16 [2, 16, 256, 22, 16, 256], P(None, 'row', None, None, 'col'), as said below
Outputs:
- factored: bfloat16 [2, 16, 256, 22, 16, 256], P(None, 'row', None, None, 'col')
Inputs may be any that keep to these rules, and one draw needn't show every extreme that they name: `matrix`: every diagonal entry of the strip is twice or more the typical size of the sum of the off-diagonal entries in its row of its block, so that factoring without pivoting is stable.
All inputs are finite; a program needn't handle non-finite values.
Results may differ from the reference program's by a relative error of at most 0.0054.
Values may be sent and summed in bfloat16 or wider, within the bound.
A program may use at most 192 MiB of HBM per device.

```python
import jax
import jax.numpy as jnp
from jax import lax

NB = 256
RB_DEV = 2
CB_DEV = 22
STEPS = 2
ROWS = 8192
ORDER = 90112
N_ROW = 16
N_COL = 16


def lax_iota(shape, dimension):
    return jax.lax.broadcasted_iota(jnp.int32, shape, dimension)


def draw_matrix(key, part):
    key = jax.random.fold_in(key, 7)
    first_key, second_key, third_key = jax.random.split(key, 3)
    shape = (RB_DEV, N_ROW, NB, CB_DEV, N_COL, NB)
    band_scale = 2.4
    entries = 0.6 * jnp.clip(jax.random.normal(first_key, shape, jnp.float32), -4.0, 4.0)
    banded = band_scale * jnp.clip(jax.random.normal(third_key, shape, jnp.float32), -4.0, 4.0)
    row_blocks = lax_iota(shape, 0) * N_ROW + lax_iota(shape, 1)
    col_blocks = lax_iota(shape, 3) * N_COL + lax_iota(shape, 4)
    inner_row = lax_iota(shape, 2)
    inner_col = lax_iota(shape, 5)
    same_block = row_blocks == col_blocks
    on_diag = same_block & (inner_row == inner_col)
    near = jnp.abs(inner_row - inner_col) <= 32
    in_band = same_block & near & (inner_row != inner_col)
    band_width = min(65, NB)
    heavy = band_scale * band_width ** 0.5 * (2.3 + 0.8 * jax.random.uniform(second_key, shape, jnp.float32))
    values = jnp.where(in_band, banded, entries)
    return jnp.where(on_diag, heavy, values).astype(jnp.bfloat16)


def setup_inputs(seed: int = 0) -> dict:
    key_of = jax.random.split(jax.random.key(seed), 2)
    matrix = draw_matrix(jax.random.fold_in(key_of[1], 71), 0)
    return {"matrix": matrix}


def product(left, right):
    return jnp.dot(left, right, precision=lax.Precision.HIGHEST)


def series_inverse(nilpotent):
    size = nilpotent.shape[0]
    ident = jnp.eye(size, dtype=nilpotent.dtype)
    result = ident + nilpotent
    power = nilpotent
    for level in range((size - 1).bit_length() - 1):
        power = product(power, power)
        result = result + product(result, power)
    return result


def unit_lower_inverse(packed):
    return series_inverse(-jnp.tril(packed, -1))


def upper_inverse(packed):
    diag_part = jnp.diagonal(packed)
    strict = jnp.triu(packed, 1) / diag_part[:, None]
    return series_inverse(-strict) / diag_part[None, :]


def lu_blocked(block):
    size = block.shape[0]
    if size <= 16:
        for column in range(size - 1):
            below = block[column + 1:, column] / block[column, column]
            block = block.at[column + 1:, column].set(below)
            block = block.at[column + 1:, column + 1:].add(-below[:, None] * block[column, column + 1:][None, :])
        return block
    half = size // 2
    top = lu_blocked(block[:half, :half])
    right = product(unit_lower_inverse(top), block[:half, half:])
    left = product(block[half:, :half], upper_inverse(top))
    rest = lu_blocked(block[half:, half:] - product(left, right))
    upper_part = jnp.concatenate([top, right], axis=1)
    lower_part = jnp.concatenate([left, rest], axis=1)
    return jnp.concatenate([upper_part, lower_part], axis=0)


def reference(matrix):
    work = matrix.reshape(ROWS, ORDER)
    row_block = jnp.arange(ROWS) // NB
    col_block = jnp.arange(ORDER) // NB
    width = NB * N_COL
    for step in range(STEPS):
        first = step * NB
        last = first + NB
        packed = lu_blocked(work[first:last, first:last].astype(jnp.float32))
        lower_half = unit_lower_inverse(packed).astype(jnp.bfloat16)
        upper_half = upper_inverse(packed).astype(jnp.bfloat16)
        lpanel = jnp.dot(work[:, first:last], upper_half, preferred_element_type=jnp.float32).astype(jnp.bfloat16)
        lpanel = jnp.where((row_block > step)[:, None], lpanel, jnp.zeros_like(lpanel))
        urow = jnp.dot(lower_half, work[first:last, :], preferred_element_type=jnp.float32).astype(jnp.bfloat16)
        urow = jnp.where((col_block > step)[None, :], urow, jnp.zeros_like(urow))
        slabs = []
        for index in range(CB_DEV):
            begin = index * width
            upper = urow[:, begin:begin + width]
            update = jnp.dot(lpanel, upper, preferred_element_type=jnp.float32)
            slabs.append((work[:, begin:begin + width].astype(jnp.float32) - update).astype(jnp.bfloat16))
        fresh = jnp.concatenate(slabs, axis=1)
        column_new = jnp.where((row_block > step)[:, None], lpanel, fresh[:, first:last])
        fresh = fresh.at[:, first:last].set(column_new)
        row_new = jnp.where((col_block > step)[None, :], urow, fresh[first:last, :])
        fresh = fresh.at[first:last, :].set(row_new)
        fresh = fresh.at[first:last, first:last].set(packed.astype(jnp.bfloat16))
        work = fresh
    return work.reshape(matrix.shape)
```

```python
import jax, jax.numpy as jnp
from jax import lax
from jax.experimental import pallas as pl
from jax.experimental.pallas import tpu as pltpu
from jax.sharding import PartitionSpec as P

NB = 256
HB = 128
BF = jnp.bfloat16
F32 = jnp.float32


def dot32(a, b):
    return jnp.dot(a, b, precision=lax.Precision.HIGHEST, preferred_element_type=F32)


def dot16(a, b):
    return jnp.dot(a, b, preferred_element_type=F32)


def pick_lane(x, lane):
    return jnp.take_along_axis(x, jnp.full(x.shape, lane, jnp.int32), axis=1)


def pick_row(x, row):
    return jnp.broadcast_to(x[row : row + 1, :], x.shape)


def eliminate(m, rows, cols):
    lane = lax.broadcasted_iota(jnp.int32, (8, HB), 1)
    sub = lax.broadcasted_iota(jnp.int32, (8, HB), 0)

    def group(g, carry):
        base = pl.multiple_of(g * 8, 8)
        own = m[pl.ds(base, 8), :]
        cb = [pick_lane(own, base + u) for u in range(8)]
        saved_row = jnp.zeros((8, HB), F32)
        saved_col = cols[pl.ds(base, 8), :]
        for t in range(8):
            here = lane == base + t
            at = sub == t
            inv = 1.0 / pick_row(cb[t], t)
            saved_row = jnp.where(at, own, saved_row)
            saved_col = jnp.where(here, jnp.where(at, inv, cb[t] * inv), saved_col)
            mult = jnp.where(at, -1.0, cb[t])
            scaled = jnp.where(here, 1.0, pick_row(own, t)) * inv
            own = jnp.where(here | at, 0.0, own) - mult * scaled
            for u in range(t + 1, 8):
                cb[u] = jnp.where(at, 0.0, cb[u]) - mult * (pick_row(cb[u], t) * inv)
        inside = (lane >= base) & (lane < base + 8)
        wr = [pick_row(own, u) for u in range(8)]
        for r in range(HB // 8):
            part = pl.ds(8 * r, 8)
            old = m[part, :]
            cols[part, :] = jnp.where(inside, old, cols[part, :])
            new = jnp.where(inside, 0.0, old)
            for u in range(8):
                new = new - pick_lane(old, base + u) * wr[u]
            m[part, :] = new
        m[pl.ds(base, 8), :] = own
        rows[pl.ds(base, 8), :] = saved_row
        cols[pl.ds(base, 8), :] = saved_col
        return carry

    lax.fori_loop(0, HB // 8, group, 0)


def pieces(m, rows, cols):
    i = lax.broadcasted_iota(jnp.int32, (HB, HB), 0)
    j = lax.broadcasted_iota(jnp.int32, (HB, HB), 1)
    near = (i // 8) == (j // 8)
    c = cols[...]
    r = rows[...]
    small = jnp.where(near & (i < j), -c, jnp.where(i == j, c, 0.0))
    far = dot32(jnp.where(near, 0.0, c), small)
    mixed = jnp.where(near, c, far)
    low = jnp.where(i > j, mixed, 0.0)
    upinv = jnp.where(i < j, -mixed, jnp.where(i == j, c, 0.0))
    lowinv = jnp.where(i > j, r, jnp.where(i == j, 1.0, 0.0))
    packed = jnp.where(i > j, low, r)
    return m[...], packed, lowinv, upinv


def factor(a, linv, uinv, packed, m, rows, cols, keep):
    lo, hi = pl.ds(0, HB), pl.ds(HB, HB)
    m[...] = a[lo, lo]
    eliminate(m, rows, cols)
    inv, pk, li, ui = pieces(m, rows, cols)
    a12, a21 = a[lo, hi], a[hi, lo]
    w = dot32(inv, a12)
    m[...] = a[hi, hi] - dot32(a21, w)
    keep[0] = w
    keep[1] = dot32(a21, inv)
    packed[lo, lo] = pk.astype(BF)
    packed[lo, hi] = dot32(li, a12).astype(BF)
    packed[hi, lo] = dot32(a21, ui).astype(BF)
    linv[lo, lo] = li.astype(BF)
    uinv[lo, lo] = ui.astype(BF)
    eliminate(m, rows, cols)
    inv, pk, li, ui = pieces(m, rows, cols)
    packed[hi, hi] = pk.astype(BF)
    linv[hi, hi] = li.astype(BF)
    uinv[hi, hi] = ui.astype(BF)
    linv[hi, lo] = (-dot32(li, keep[1])).astype(BF)
    uinv[lo, hi] = (-dot32(keep[0], ui)).astype(BF)
    linv[lo, hi] = jnp.zeros((HB, HB), BF)
    uinv[hi, lo] = jnp.zeros((HB, HB), BF)

MESH = pl.DeviceIdType.MESH
NCOL = 22
PER = 2
NCH = NCOL * PER
CH = NB // PER


def comm(work, ring, corner, panel, rs, rr, ss, sr, ps, pr, ks, kr, loc):
    row = lax.axis_index("row")
    col = lax.axis_index("col")
    z, core = row // 2, row % 2
    x, y = col // 4, col % 4
    way = 1 - 2 * core
    dist = (z * way + 8) % 8
    nxt = ((z + way + 8) % 8) * 2 + core
    prv = ((z - way + 8) % 8) * 2 + core
    sib = row + way

    def at(xx, yy):
        return ((xx + 4) % 4) * 4 + (yy + 4) % 4

    barrier = pltpu.get_barrier_semaphore()
    for dev in (
        (nxt, col), (prv, col), (sib, col),
        (row, at(x + 1, y)), (row, at(x - 1, y)), (row, at(x, y + 1)), (row, at(x, y - 1)),
    ):
        pl.semaphore_signal(barrier, inc=1, device_id=dev, device_id_type=MESH)
    pl.semaphore_wait(barrier, 7)

    def piece(ref, n):
        return ref.at[n // PER, pl.ds(pl.multiple_of((n % PER) * CH, CH), CH), :]

    def remote(src, dst, send, recv, dev):
        return pltpu.make_async_remote_copy(
            src_ref=src, dst_ref=dst, send_sem=send, recv_sem=recv, device_id=dev, device_id_type=MESH
        )

    def ahead(n, src):
        return remote(piece(src, n), piece(ring.at[core], n), rs.at[n], rr.at[n], (nxt, col))

    def across(n, src):
        return remote(piece(src, n), piece(ring.at[core], n), ss.at[n], sr.at[n], (sib, col))

    mine = work.at[0]
    fill = pltpu.make_async_copy(mine, ring.at[core], loc.at[0])

    @pl.when(dist == 0)
    def _():
        fill.start()

    def step(n):
        @pl.when(dist == 0)
        def _():
            ahead(n, mine).start()
            across(n, mine).start()

        @pl.when(dist > 0)
        def _():
            ahead(n, ring.at[core]).wait_recv()

            @pl.when(dist < 7)
            def _():
                ahead(n, ring.at[core]).start()

            across(n, ring.at[core]).start()

    def steps(first, last):
        lax.fori_loop(first, last, lambda n, c: (step(n), c)[1], 0)

    def item(s, q):
        return corner.at[core, s] if q == 0 else panel.at[s, q - 1]

    def hop(s, q, slot, src, dev):
        return remote(src, item(s, q), ps.at[s, q, slot], pr.at[s, q], (row, dev))

    rel = [(y - s + 4) % 4 for s in range(2)]
    children = [
        lambda s: ((x == 0) & (rel[s] < 2), at(x, y + 1)),
        lambda s: ((x == 0) & (rel[s] == 0), at(x, y - 1)),
        lambda s: (x < 2, at(x + 1, y)),
        lambda s: (x == 0, at(x - 1, y)),
    ]

    def is_root(s):
        return (x == 0) & (rel[s] == 0)

    def spread(s, q, src):
        for slot, child in enumerate(children):
            cond, dev = child(s)

            @pl.when(cond)
            def _(slot=slot, dev=dev):
                hop(s, q, slot, src, dev).start()

    def twin(s, src):
        return remote(src, corner.at[core, s], ks.at[s], kr.at[s], (sib, col))

    def own(s, q, src):
        return pltpu.make_async_copy(src, item(s, q), loc.at[1 + s * 3 + q])

    def send(s, q, src):
        own(s, q, src).start()
        spread(s, q, src)
        if q == 0:
            twin(s, src).start()

    def relay(s, q):
        @pl.when(jnp.logical_not(is_root(s)))
        def _():
            hop(s, q, 0, item(s, q), col).wait_recv()
            spread(s, q, item(s, q))
            if q == 0:
                twin(s, item(s, q)).start()

    steps(0, PER)
    for s in range(2):
        @pl.when(is_root(s) & (dist == 0))
        def _(s=s):
            send(s, 0, mine.at[0])

        @pl.when(is_root(s) & (dist > 0))
        def _(s=s):
            send(s, 0, ring.at[core, 0])

        @pl.when(is_root(s))
        def _(s=s):
            for k in range(2):
                send(s, 1 + k, work.at[k, 0])

    steps(PER, PER + 4)
    for s in range(2):
        relay(s, 0)
    steps(PER + 4, PER + 12)
    for s in range(2):
        for k in range(2):
            relay(s, 1 + k)
    steps(PER + 12, NCH)

    @pl.when(dist == 0)
    def _():
        fill.wait()

    def drain(n, c):
        @pl.when(dist < 7)
        def _():
            ahead(n, ring.at[core]).wait_send()

        across(n, ring.at[core]).wait_send()
        other = piece(ring.at[1 - core], n)
        remote(other, other, ss.at[n], sr.at[n], (sib, col)).wait_recv()
        return c

    lax.fori_loop(0, NCH, drain, 0)
    for s in range(2):
        twin(s, corner.at[core, s]).wait_send()
        remote(corner.at[1 - core, s], corner.at[1 - core, s], ks.at[s], kr.at[s], (sib, col)).wait_recv()
        for q in range(3):
            for slot, child in enumerate(children):
                cond, dev = child(s)

                @pl.when(cond)
                def _(s=s, q=q, slot=slot, dev=dev):
                    hop(s, q, slot, item(s, q), dev).wait_send()

            @pl.when(is_root(s))
            def _(s=s, q=q):
                own(s, q, item(s, q)).wait()


def gather(work):
    block = jax.ShapeDtypeStruct
    hbm = pl.BlockSpec(memory_space=pl.ANY)
    dma = pltpu.SemaphoreType.DMA
    return pl.pallas_call(
        comm,
        out_shape=(
            block((2, NCOL, NB, NB), BF),
            block((2, 2, NB, NB), BF),
            block((2, 2, NB, NB), BF),
        ),
        in_specs=[hbm],
        out_specs=(hbm, hbm, hbm),
        scratch_shapes=[
            dma((NCH,)), dma((NCH,)), dma((NCH,)), dma((NCH,)),
            dma((2, 3, 4)), dma((2, 3)), dma((2,)), dma((2,)), dma((7,)),
        ],
        compiler_params=pltpu.CompilerParams(collective_id=0, has_side_effects=True),
        name="gather",
    )(work)


def small(corner, panel, linv, low, pan, packed, a, uinv, keep, urow, m, rows, cols, part):
    row = lax.axis_index("row")

    def solve_panel(s, k, block):
        keep_it = (k * 16 + row) > s
        out = dot16(block, uinv[...]).astype(BF)
        pan[s, k] = jnp.where(keep_it, out, jnp.zeros_like(out))

    a[...] = corner[0, 0].astype(F32)
    factor(a, linv.at[0], uinv, packed.at[0], m, rows, cols, part)
    for k in range(2):
        solve_panel(0, k, panel[0, k])
    low[...] = dot16(corner[1, 0], uinv[...]).astype(BF)
    urow[...] = dot16(linv[0], corner[0, 1]).astype(BF)
    a[...] = (corner[1, 1].astype(F32) - dot16(low[...], urow[...])).astype(BF).astype(F32)
    factor(a, linv.at[1], uinv, packed.at[1], m, rows, cols, part)
    for k in range(2):
        block = (panel[1, k].astype(F32) - dot16(pan[0, k], urow[...])).astype(BF)
        solve_panel(1, k, block)


def factors(corner, panel):
    block = jax.ShapeDtypeStruct
    vm = pl.BlockSpec(memory_space=pltpu.VMEM)
    return pl.pallas_call(
        small,
        out_shape=(
            block((2, NB, NB), BF),
            block((NB, NB), BF),
            block((2, 2, NB, NB), BF),
            block((2, NB, NB), BF),
        ),
        in_specs=[vm] * 2,
        out_specs=(vm,) * 4,
        scratch_shapes=[
            pltpu.VMEM((NB, NB), F32),
            pltpu.VMEM((NB, NB), BF),
            pltpu.VMEM((NB, NB), BF),
            pltpu.VMEM((NB, NB), BF),
            pltpu.VMEM((HB, HB), F32),
            pltpu.VMEM((HB, HB), F32),
            pltpu.VMEM((HB, HB), F32),
            pltpu.VMEM((2, HB, HB), F32),
        ],
        name="factors",
    )(corner, panel)


def bulk(work, ring, linv, low, pan, packed, out):
    row = lax.axis_index("row")
    col = lax.axis_index("col")
    j = pl.program_id(0)
    for b in range(WIDE):
        jj = j * WIDE + b
        cblk = jj * 16 + col
        u0 = dot16(linv[0], ring[0, b]).astype(BF)
        u0 = jnp.where(cblk > 0, u0, jnp.zeros_like(u0))
        second = (ring[1, b].astype(F32) - dot16(low[...], u0)).astype(BF)
        u1 = dot16(linv[1], second).astype(BF)
        u1 = jnp.where(cblk > 1, u1, jnp.zeros_like(u1))
        for k in range(2):
            rblk = k * 16 + row
            new = (work[k, b].astype(F32) - dot16(pan[0, k], u0)).astype(BF)
            new = (new.astype(F32) - dot16(pan[1, k], u1)).astype(BF)
            out[k, b] = new
            if k == 0:
                @pl.when((rblk == 0) & (cblk > 0))
                def _(k=k, b=b):
                    out[k, b] = u0

                @pl.when((rblk == 1) & (cblk > 1))
                def _(k=k, b=b):
                    out[k, b] = u1

            if b == 0:
                for s in range(2):
                    @pl.when((cblk == s) & (rblk > s))
                    def _(k=k, b=b, s=s):
                        out[k, b] = pan[s, k]

                    @pl.when((cblk == s) & (rblk == s))
                    def _(k=k, b=b, s=s):
                        out[k, b] = packed[s]


WIDE = 2


def update(work, ring, linv, low, pan, packed):
    full = lambda *shape: pl.BlockSpec(shape, lambda j: (0,) * len(shape))
    stream = pl.BlockSpec((2, WIDE, NB, NB), lambda j: (0, j, 0, 0))
    return pl.pallas_call(
        bulk,
        grid=(NCOL // WIDE,),
        out_shape=jax.ShapeDtypeStruct(work.shape, BF),
        in_specs=[
            stream, stream, full(2, NB, NB), full(NB, NB), full(2, 2, NB, NB), full(2, NB, NB),
        ],
        out_specs=stream,
        name="bulk",
    )(work, ring, linv, low, pan, packed)


def local(matrix):
    work = matrix.transpose(0, 1, 3, 4, 2, 5).reshape(2, NCOL, NB, NB)
    ring, corner, panel = gather(work)
    linv, low, pan, packed = factors(corner, panel)
    out = update(work, ring, linv, low, pan, packed)
    return out.reshape(2, 1, NCOL, 1, NB, NB).transpose(0, 1, 4, 2, 3, 5)


def solution(mesh):
    spec = P(None, "row", None, None, "col", None)
    return jax.shard_map(local, mesh=mesh, in_specs=(spec,), out_specs=spec, check_vma=False)
```

```python
import functools

import jax
import jax.numpy as jnp
from jax import lax
from jax.experimental import pallas as pl
from jax.experimental.pallas import tpu as pltpu
from jax.sharding import PartitionSpec as P

NB = 256
HB = 128
BF = jnp.bfloat16
F32 = jnp.float32


def dot32(a, b):
    return jnp.dot(a, b, precision=lax.Precision.HIGHEST, preferred_element_type=F32)


def dot16(a, b):
    return jnp.dot(a, b, preferred_element_type=F32)


def pick_lane(x, lane):
    return jnp.take_along_axis(x, jnp.full(x.shape, lane, jnp.int32), axis=1)


def pick_row(x, row):
    return jnp.broadcast_to(x[row : row + 1, :], x.shape)


def eliminate(m, rows, cols):
    lane = lax.broadcasted_iota(jnp.int32, (8, HB), 1)
    sub = lax.broadcasted_iota(jnp.int32, (8, HB), 0)

    def group(g, carry):
        base = pl.multiple_of(g * 8, 8)
        own = m[pl.ds(base, 8), :]
        cb = [pick_lane(own, base + u) for u in range(8)]
        saved_row = jnp.zeros((8, HB), F32)
        saved_col = cols[pl.ds(base, 8), :]
        for t in range(8):
            here = lane == base + t
            at = sub == t
            inv = 1.0 / pick_row(cb[t], t)
            saved_row = jnp.where(at, own, saved_row)
            saved_col = jnp.where(here, jnp.where(at, inv, cb[t] * inv), saved_col)
            mult = jnp.where(at, -1.0, cb[t])
            scaled = jnp.where(here, 1.0, pick_row(own, t)) * inv
            own = jnp.where(here | at, 0.0, own) - mult * scaled
            for u in range(t + 1, 8):
                cb[u] = jnp.where(at, 0.0, cb[u]) - mult * (pick_row(cb[u], t) * inv)
        inside = (lane >= base) & (lane < base + 8)
        wr = [pick_row(own, u) for u in range(8)]
        for r in range(HB // 8):
            part = pl.ds(8 * r, 8)
            old = m[part, :]
            cols[part, :] = jnp.where(inside, old, cols[part, :])
            new = jnp.where(inside, 0.0, old)
            for u in range(8):
                new = new - pick_lane(old, base + u) * wr[u]
            m[part, :] = new
        m[pl.ds(base, 8), :] = own
        rows[pl.ds(base, 8), :] = saved_row
        cols[pl.ds(base, 8), :] = saved_col
        return carry

    lax.fori_loop(0, HB // 8, group, 0)


def pieces(m, rows, cols):
    i = lax.broadcasted_iota(jnp.int32, (HB, HB), 0)
    j = lax.broadcasted_iota(jnp.int32, (HB, HB), 1)
    near = (i // 8) == (j // 8)
    c = cols[...]
    r = rows[...]
    small = jnp.where(near & (i < j), -c, jnp.where(i == j, c, 0.0))
    far = dot32(jnp.where(near, 0.0, c), small)
    mixed = jnp.where(near, c, far)
    low = jnp.where(i > j, mixed, 0.0)
    upinv = jnp.where(i < j, -mixed, jnp.where(i == j, c, 0.0))
    lowinv = jnp.where(i > j, r, jnp.where(i == j, 1.0, 0.0))
    packed = jnp.where(i > j, low, r)
    return m[...], packed, lowinv, upinv


def factor(a, linv, uinv, packed, m, rows, cols, keep):
    lo, hi = pl.ds(0, HB), pl.ds(HB, HB)
    m[...] = a[lo, lo]
    eliminate(m, rows, cols)
    inv, pk, li, ui = pieces(m, rows, cols)
    a12, a21 = a[lo, hi], a[hi, lo]
    w = dot32(inv, a12)
    m[...] = a[hi, hi] - dot32(a21, w)
    keep[0] = w
    keep[1] = dot32(a21, inv)
    packed[lo, lo] = pk.astype(BF)
    packed[lo, hi] = dot32(li, a12).astype(BF)
    packed[hi, lo] = dot32(a21, ui).astype(BF)
    linv[lo, lo] = li.astype(BF)
    uinv[lo, lo] = ui.astype(BF)
    eliminate(m, rows, cols)
    inv, pk, li, ui = pieces(m, rows, cols)
    packed[hi, hi] = pk.astype(BF)
    linv[hi, hi] = li.astype(BF)
    uinv[hi, hi] = ui.astype(BF)
    linv[hi, lo] = (-dot32(li, keep[1])).astype(BF)
    uinv[lo, hi] = (-dot32(keep[0], ui)).astype(BF)
    linv[lo, hi] = jnp.zeros((HB, HB), BF)
    uinv[hi, lo] = jnp.zeros((HB, HB), BF)

MESH = pl.DeviceIdType.MESH
NCOL = 22
PER = 2
NCH = NCOL * PER
CH = NB // PER
NZ = 8
TICKS = 82
PACE = 4


def lag(d):
    return 5 * d


def comm(
    work, ring, q_out, patch,
    rs, rr, ss, sr, kz, kc, ksend, kloc, pr, pt, psend, ploc, loc, fs, fr,
    kb, pb, fb, pk1, pan, a, low, m, rows, cols, part,
):
    row = lax.axis_index("row")
    col = lax.axis_index("col")
    z, core = row // 2, row % 2
    x, y = col // 4, col % 4
    sib = row + 1 - 2 * core

    def pos(xx, yy):
        return ((xx + 4) % 4) * 4 + (yy + 4) % 4

    def rowof(zz, cc):
        return ((zz + NZ) % NZ) * 2 + cc

    def remote(src, dst, send, recv, dev):
        return pltpu.make_async_remote_copy(
            src_ref=src, dst_ref=dst, send_sem=send, recv_sem=recv, device_id=dev, device_id_type=MESH
        )

    barrier = pltpu.get_barrier_semaphore()

    def greet(dev):
        pl.semaphore_signal(barrier, inc=1, device_id=dev, device_id_type=MESH)

    greet((sib, col))

    @pl.when(core == 0)
    def _():
        greet((rowof(z + 1, 0), col))
        greet((rowof(z - 1, 0), col))
        for step in (1, 2, 3):
            greet((row, pos(x, y + step)))
        greet((row, pos(x + 1, y)))
        greet((row, pos(x - 1, y)))

        @pl.when(x == 0)
        def _():
            for xx in (1, 2, 3):
                greet((sib, pos(xx, y)))

        @pl.when((z == 1) | (z == NZ - 1))
        def _():
            greet((rowof(0, 1), col))

        pl.semaphore_wait(
            barrier, 8 + jnp.where(x == 0, 3, 0) + jnp.where((z == 1) | (z == NZ - 1), 1, 0)
        )

    @pl.when(core == 1)
    def _():
        @pl.when(x != 0)
        def _():
            greet((sib, pos(0, y)))

        @pl.when(z == 0)
        def _():
            greet((rowof(1, 0), col))
            greet((rowof(NZ - 1, 0), col))

        pl.semaphore_wait(barrier, 1 + jnp.where(x != 0, 1, 0) + jnp.where(z == 0, 2, 0))

    dist = [z, (NZ - z) % NZ]
    after = [rowof(z + 1, 0), rowof(z - 1, 0)]
    short = col < 2
    first = jnp.where(short, PER, 0)
    extra = jnp.where(short, 2, 0)

    def piece(ref, n):
        return ref.at[n // PER, pl.ds(pl.multiple_of((n % PER) * CH, CH), CH), :]

    def ahead(r, n, src):
        return remote(piece(src, n), piece(ring.at[r], n), rs.at[r, n], rr.at[r, n], (after[r], col))

    def across(r, n, src):
        return remote(piece(src, n), piece(ring.at[r], n), ss.at[r, n], sr.at[r, n], (sib, col))

    mine = work.at[0]
    fill = pltpu.make_async_copy(mine, ring.at[core], loc.at[0])

    def loop(lo, hi, body):
        lax.fori_loop(lo, hi, lambda n, c: (body(n), c)[1], 0)

    def half(ref, h):
        return ref.at[pl.ds(h * HB, HB), :]

    def kpiece(c, s, h):
        return half(kb.at[c, s], h)

    def corner_sends(c, s):
        root = y == s
        return [
            (root & (z < 4) & (((z > 0) if c else (z >= 0))), (rowof(z + 1, 0), col), 0),
            (root & ((z > 5) if c else ((z > 5) | (z == 0))), (rowof(z - 1, 0), col), 0),
            (root, (row, pos(x, y + 2)), 0),
            (root, (row, pos(x, y + 1)), 0),
            (root, (row, pos(x, y + 3)), 0),
            (None, (sib, pos(x + 2, y)), 1),
            (None, (sib, pos(x + 1, y)), 1),
            (None, (sib, pos(x + 3, y)), 1),
            (None, (sib, col), 1),
        ]

    def each(c, s, h, act):
        for slot, (cond, dev, to) in enumerate(corner_sends(c, s)):
            sem = (kc if to else kz).at[c, s, h]
            copy = remote(kpiece(c, s, h), kpiece(c, s, h), ksend.at[c, s, h, slot], sem, dev)
            if cond is None:
                act(copy)
            else:
                pl.when(cond)(functools.partial(act, copy))

    def kwait(c, s, h, sem):
        remote(kpiece(c, s, h), kpiece(c, s, h), ksend.at[c, s, h, 0], sem.at[c, s, h], (row, col)).wait_recv()

    def corner_event(c, s):
        for h in range(2):
            if c == 0:
                @pl.when((z == 0) & (y == s))
                def _():
                    pltpu.make_async_copy(half(mine.at[0], h), kpiece(c, s, h), kloc.at[s, h]).wait()

                @pl.when((z > 0) | (y != s))
                def _():
                    kwait(c, s, h, kz)
            else:
                kwait(c, s, h, kz)
            each(c, s, h, lambda copy: copy.start())

    rel = [(y - s + 4) % 4 for s in range(2)]

    def is_root(s):
        return (x == 0) & (rel[s] == 0)

    def panel_sends(c, s):
        return [
            ((x == 0) & (rel[s] < 2), (row, pos(x, y + 1))),
            ((x == 0) & (rel[s] == 0), (row, pos(x, y - 1))),
            (x < 2, (row, pos(x + 1, y))),
            (x == 0, (row, pos(x - 1, y))),
        ]

    def each_panel(c, s, k, act):
        item = pb.at[c, s, k]
        for slot, (cond, dev) in enumerate(panel_sends(c, s)):
            pl.when(cond)(
                functools.partial(act, remote(item, item, psend.at[c, s, k, slot], pr.at[c, s, k], dev))
            )
        if c == 1:
            pl.when(jnp.logical_not(is_root(s)))(
                functools.partial(act, remote(item, item, psend.at[c, s, k, 4], pt.at[s, k], (sib, col)))
            )

    def own_panel(s, k):
        return pltpu.make_async_copy(work.at[k, 0], pb.at[core, s, k], ploc.at[s, k])

    def panel_event(c, s, k):
        item = pb.at[c, s, k]
        arrive = remote(item, item, psend.at[c, s, k, 0], pr.at[c, s, k], (row, col))
        if c == 0:
            @pl.when(is_root(s))
            def _():
                own_panel(s, k).wait()

            @pl.when(jnp.logical_not(is_root(s)))
            def _():
                arrive.wait_recv()
        else:
            arrive.wait_recv()
        each_panel(c, s, k, lambda copy: copy.start())

    def solve(s, k, block):
        out = dot16(block, fb[4 * s + 1]).astype(BF)
        pan[s, k] = jnp.where(k * 16 + row > s, out, jnp.zeros_like(out))

    def own_factors(c, recv):
        for k in range(2):
            solve(0, k, pb[c, 0, k])
        for k in range(2):
            block = (pb[c, 1, k].astype(F32) - dot16(pan[0, k], fb[3])).astype(BF)
            solve(1, k, block)
            left = dot16(pan[0, k], fb[0]) + dot16(pan[1, k], fb[6])
            right = dot16(pan[1, k], fb[4])
            if k == 0:
                left = jnp.where(row == c, -(fb[0] if c == 0 else fb[6]).astype(F32), left)
                right = jnp.where(row == c, jnp.zeros_like(right) if c == 0 else -fb[4].astype(F32), right)
            q_out[k, :, pl.ds(0, NB)] = left.astype(BF)
            q_out[k, :, pl.ds(NB, NB)] = right.astype(BF)
            if k == 0 and c == 0:
                patch[k] = jnp.where(
                    row == 0,
                    jnp.where(col == 0, fb[2], fb[3]),
                    jnp.where(col == 0, pan[0, k], pan[1, k]),
                )
            elif k == 0:
                patch[k] = jnp.where(
                    (row == 1) & (col != 0), pk1[...], jnp.where(col == 0, pan[0, k], pan[1, k])
                )
            else:
                patch[k] = jnp.where(col == 0, pan[0, k], pan[1, k])

    def give(i):
        return remote(fb.at[i], fb.at[i], fs.at[i], fr.at[i], (sib, col))

    @pl.when(core == 0)
    def _():
        @pl.when((z == 0) & (x == 0) & (y < 2))
        def _():
            for s in range(2):
                for h in range(2):
                    @pl.when(y == s)
                    def _():
                        pltpu.make_async_copy(half(mine.at[0], h), kpiece(0, s, h), kloc.at[s, h]).start()

        for s in range(2):
            @pl.when(is_root(s))
            def _():
                for k in range(2):
                    own_panel(s, k).start()

        @pl.when(z == 0)
        def _():
            fill.start()

        start = lag(jnp.minimum(z, NZ - z))

        def tick(t):
            for c in range(2):
                for s in range(2):
                    when = start + jnp.where(y == s, 2 * c + 1, 3 * c + 6)

                    @pl.when((x == 0) & (t == when))
                    def _():
                        corner_event(c, s)

            for r in range(2):
                n = t - lag(dist[r]) - extra

                @pl.when((dist[r] > 0) & (n >= first) & (n < NCH))
                def _():
                    ahead(r, n, ring.at[r]).wait_recv()

                    @pl.when(dist[r] < NZ - 1)
                    def _():
                        ahead(r, n, ring.at[r]).start()

                    across(r, n, ring.at[r]).start()

            n = t - extra

            @pl.when((z == 0) & (n >= first) & (n < NCH))
            def _():
                ahead(0, n, mine).start()
                across(0, n, mine).start()

                @pl.when(n >= first + PACE)
                def _():
                    ahead(0, n - PACE, mine).wait_send()

            for s in range(2):
                hops = jnp.where(x == 0, 0, jnp.where(x == 2, 4, 3))
                hops = jnp.where(x == 0, jnp.where(rel[s] == 2, 2, jnp.minimum(rel[s], 1)), hops)
                for k in range(2):
                    for c in range(2):
                        @pl.when(t == start + 9 + 4 * hops + 2 * (4 * k + 2 * s + c))
                        def _():
                            panel_event(c, s, k)

        loop(0, TICKS, tick)
        for i in range(7):
            give(i).wait_recv()
        own_factors(0, None)

        for r in range(2):
            @pl.when((dist[r] > 0) & (dist[r] < NZ - 1))
            def _():
                loop(first, NCH, lambda n: ahead(r, n, mine).wait_send())

            @pl.when(dist[r] > 0)
            def _():
                loop(first, NCH, lambda n: across(r, n, mine).wait_send())

        @pl.when(z == 0)
        def _():
            fill.wait()
            loop(NCH - PACE, NCH, lambda n: ahead(0, n, mine).wait_send())
            loop(first, NCH, lambda n: across(0, n, mine).wait_send())
            loop(first, NCH, lambda n: across(1, n, mine).wait_recv())

        @pl.when(x == 0)
        def _():
            for c in range(2):
                for s in range(2):
                    for h in range(2):
                        each(c, s, h, lambda copy: copy.wait_send())

        for c in range(2):
            for s in range(2):
                for k in range(2):
                    each_panel(c, s, k, lambda copy: copy.wait_send())

    @pl.when(core == 1)
    def _():
        def root_sends(s, act):
            for h in range(2):
                for slot, dev in enumerate(((rowof(1, 0), col), (rowof(NZ - 1, 0), col), (sib, col))):
                    act(remote(
                        half(mine.at[0], h), kpiece(1, s, h), ksend.at[1, s, h, slot], kz.at[1, s, h], dev
                    ))

        def panel_give(s, k):
            return remote(work.at[k, 0], pb.at[1, s, k], psend.at[1, s, k, 0], pr.at[1, s, k], (sib, col))

        for s in range(2):
            @pl.when(is_root(s) & (z == 0))
            def _():
                root_sends(s, lambda copy: copy.start())

            @pl.when(is_root(s))
            def _():
                for k in range(2):
                    panel_give(s, k).start()
                    own_panel(s, k).start()

        @pl.when(z == 0)
        def _():
            fill.start()

            def both(n):
                ahead(1, n, mine).start()
                across(1, n, mine).start()

            loop(first, NCH, both)

        for h in range(2):
            kwait(0, 0, h, kc)
        a[...] = kb[0, 0].astype(F32)
        factor(a, fb.at[0], fb.at[1], fb.at[2], m, rows, cols, part)
        for h in range(2):
            kwait(1, 0, h, kc)
            kwait(0, 1, h, kc)
            kwait(1, 1, h, kc)
        low[...] = dot16(kb[1, 0], fb[1]).astype(BF)
        fb[3] = dot16(fb[0], kb[0, 1]).astype(BF)
        for i in range(4):
            give(i).start()
        a[...] = (kb[1, 1].astype(F32) - dot16(low[...], fb[3])).astype(BF).astype(F32)
        factor(a, fb.at[4], fb.at[5], pk1, m, rows, cols, part)
        give(4).start()
        give(5).start()
        mid = dot16(low[...], fb[0]).astype(BF)
        fb[6] = (-dot16(fb[4], mid)).astype(BF)
        give(6).start()
        for s in range(2):
            for k in range(2):
                @pl.when(is_root(s))
                def _():
                    own_panel(s, k).wait()

                @pl.when(jnp.logical_not(is_root(s)))
                def _():
                    item = pb.at[1, s, k]
                    remote(item, item, psend.at[1, s, k, 4], pt.at[s, k], (sib, col)).wait_recv()
        own_factors(1, None)

        for i in range(7):
            give(i).wait_send()
        for s in range(2):
            @pl.when(is_root(s) & (z == 0))
            def _():
                root_sends(s, lambda copy: copy.wait_send())

            @pl.when(is_root(s))
            def _():
                for k in range(2):
                    panel_give(s, k).wait_send()

        loop(first, NCH, lambda n: across(0, n, mine).wait_recv())

        @pl.when(z == 0)
        def _():
            fill.wait()
            loop(first, NCH, lambda n: ahead(1, n, mine).wait_send())
            loop(first, NCH, lambda n: across(1, n, mine).wait_send())

        @pl.when(z > 0)
        def _():
            loop(first, NCH, lambda n: across(1, n, mine).wait_recv())


def gather(work):
    block = jax.ShapeDtypeStruct
    hbm = pl.BlockSpec(memory_space=pl.ANY)
    vm = pl.BlockSpec(memory_space=pltpu.VMEM)
    dma = pltpu.SemaphoreType.DMA
    mem = pltpu.VMEM
    return pl.pallas_call(
        comm,
        out_shape=(
            block((2, NCOL, NB, NB), BF),
            block((2, NB, 2 * NB), BF),
            block((2, NB, NB), BF),
        ),
        in_specs=[pl.BlockSpec(memory_space=pltpu.HBM)],
        out_specs=(hbm, vm, vm),
        scratch_shapes=[
            dma((2, NCH)), dma((2, NCH)), dma((2, NCH)), dma((2, NCH)),
            dma((2, 2, 2)), dma((2, 2, 2)), dma((2, 2, 2, 9)), dma((2, 2)),
            dma((2, 2, 2)), dma((2, 2)), dma((2, 2, 2, 5)), dma((2, 2)),
            dma((1,)), dma((7,)), dma((7,)),
            mem((2, 2, NB, NB), BF),
            mem((2, 2, 2, NB, NB), BF),
            mem((7, NB, NB), BF),
            mem((NB, NB), BF),
            mem((2, 2, NB, NB), BF),
            mem((NB, NB), F32),
            mem((NB, NB), BF),
            mem((HB, HB), F32),
            mem((HB, HB), F32),
            mem((HB, HB), F32),
            mem((2, HB, HB), F32),
        ],
        compiler_params=pltpu.CompilerParams(
            collective_id=0, has_side_effects=True, vmem_limit_bytes=32 << 20
        ),
        name="gather",
    )(work)


WIDE = 2


def bulk(work, ring, q, patch, out):
    row = lax.axis_index("row")
    col = lax.axis_index("col")
    j = pl.program_id(0)
    for b in range(WIDE):
        top, bottom = ring[0, b], ring[1, b]
        for k in range(2):
            change = dot16(q[k, :, :NB], top) + dot16(q[k, :, NB:], bottom)
            base = work[k, b].astype(F32)
            if k == 0:
                base = jnp.where(row < 2, jnp.zeros_like(base), base)
            out[k, b] = (base - change).astype(BF)

    @pl.when((j == 0) & (col < 2))
    def _():
        for k in range(2):
            out[k, 0] = patch[k]


def update(work, ring, q, patch):
    full = lambda *shape: pl.BlockSpec(shape, lambda j: (0,) * len(shape))
    stream = pl.BlockSpec((2, WIDE, NB, NB), lambda j: (0, j, 0, 0))
    return pl.pallas_call(
        bulk,
        grid=(NCOL // WIDE,),
        out_shape=jax.ShapeDtypeStruct(work.shape, BF),
        in_specs=[stream, stream, full(2, NB, 2 * NB), full(2, NB, NB)],
        out_specs=stream,
        compiler_params=pltpu.CompilerParams(vmem_limit_bytes=32 << 20),
        name="bulk",
    )(work, ring, q, patch)


def local(matrix):
    work = matrix.transpose(0, 1, 3, 4, 2, 5).reshape(2, NCOL, NB, NB)
    ring, q, patch = gather(work)
    out = update(work, ring, q, patch)
    return out.reshape(2, 1, NCOL, 1, NB, NB).transpose(0, 1, 4, 2, 3, 5)


def solution(mesh):
    spec = P(None, "row", None, None, "col", None)
    return jax.shard_map(local, mesh=mesh, in_specs=(spec,), out_specs=spec, check_vma=False)
```

```python
import functools

import jax
import jax.numpy as jnp
from jax import lax
from jax.experimental import pallas as pl
from jax.experimental.pallas import tpu as pltpu
from jax.sharding import PartitionSpec as P

NB = 256
HB = 128
BF = jnp.bfloat16
F32 = jnp.float32


def dot32(a, b):
    return jnp.dot(a, b, precision=lax.Precision.HIGHEST, preferred_element_type=F32)


def dot16(a, b):
    return jnp.dot(a, b, preferred_element_type=F32)


def pick_lane(x, lane):
    return jnp.take_along_axis(x, jnp.full(x.shape, lane, jnp.int32), axis=1)


def pick_row(x, row):
    return jnp.broadcast_to(x[row : row + 1, :], x.shape)


def eliminate(m, rows, cols):
    lane = lax.broadcasted_iota(jnp.int32, (8, HB), 1)
    sub = lax.broadcasted_iota(jnp.int32, (8, HB), 0)
    wide = lax.broadcasted_iota(jnp.int32, (HB, HB), 1)
    tall = lax.broadcasted_iota(jnp.int32, (HB, HB), 0)

    def group(g, carry):
        base = pl.multiple_of(g * 8, 8)
        own = m[pl.ds(base, 8), :]
        old = m[...]
        inside = (wide >= base) & (wide < base + 8)
        taken = jnp.where(inside, old, 0.0)
        hi = taken.astype(BF)
        lo = (taken - hi.astype(F32)).astype(BF)
        cb = [pick_lane(own, base + u) for u in range(8)]
        saved_row = jnp.zeros((8, HB), F32)
        saved_col = cols[pl.ds(base, 8), :]
        for t in range(8):
            here = lane == base + t
            at = sub == t
            inv = 1.0 / pick_row(cb[t], t)
            saved_row = jnp.where(at, own, saved_row)
            saved_col = jnp.where(here, jnp.where(at, inv, cb[t] * inv), saved_col)
            mult = jnp.where(at, -1.0, cb[t])
            scaled = jnp.where(here, 1.0, pick_row(own, t)) * inv
            own = jnp.where(here | at, 0.0, own) - mult * scaled
            for u in range(t + 1, 8):
                cb[u] = jnp.where(at, 0.0, cb[u]) - mult * (pick_row(cb[u], t) * inv)
        cols[...] = jnp.where(inside, old, cols[...])
        w = jnp.where((tall >= base) & (tall < base + 8), jnp.concatenate([own] * 16, 0), 0.0)
        wh = w.astype(BF)
        wl = (w - wh.astype(F32)).astype(BF)
        right = jnp.concatenate(
            [jnp.concatenate([wh, wl], 1), jnp.concatenate([wh, jnp.zeros_like(wl)], 1)], 0
        )
        both = dot16(jnp.concatenate([hi, lo], 1), right)
        m[...] = jnp.where(inside, 0.0, old) - (both[:, :HB] + both[:, HB:])
        m[pl.ds(base, 8), :] = own
        rows[pl.ds(base, 8), :] = saved_row
        cols[pl.ds(base, 8), :] = saved_col
        return carry

    lax.fori_loop(0, HB // 8, group, 0)


def pieces(m, rows, cols):
    i = lax.broadcasted_iota(jnp.int32, (HB, HB), 0)
    j = lax.broadcasted_iota(jnp.int32, (HB, HB), 1)
    near = (i // 8) == (j // 8)
    c = cols[...]
    r = rows[...]
    small = jnp.where(near & (i < j), -c, jnp.where(i == j, c, 0.0))
    far = dot32(jnp.where(near, 0.0, c), small)
    mixed = jnp.where(near, c, far)
    low = jnp.where(i > j, mixed, 0.0)
    upinv = jnp.where(i < j, -mixed, jnp.where(i == j, c, 0.0))
    lowinv = jnp.where(i > j, r, jnp.where(i == j, 1.0, 0.0))
    packed = jnp.where(i > j, low, r)
    return m[...], packed, lowinv, upinv


def factor(a, linv, uinv, packed, m, rows, cols, keep, between=None):
    lo, hi = pl.ds(0, HB), pl.ds(HB, HB)
    m[...] = a[lo, lo]
    eliminate(m, rows, cols)
    if between is not None:
        between()
    inv, pk, li, ui = pieces(m, rows, cols)
    a12, a21 = a[lo, hi], a[hi, lo]
    w = dot32(inv, a12)
    m[...] = a[hi, hi] - dot32(a21, w)
    keep[0] = w
    keep[1] = dot32(a21, inv)
    packed[lo, lo] = pk.astype(BF)
    packed[lo, hi] = dot32(li, a12).astype(BF)
    packed[hi, lo] = dot32(a21, ui).astype(BF)
    linv[lo, lo] = li.astype(BF)
    uinv[lo, lo] = ui.astype(BF)
    eliminate(m, rows, cols)
    inv, pk, li, ui = pieces(m, rows, cols)
    packed[hi, hi] = pk.astype(BF)
    linv[hi, hi] = li.astype(BF)
    uinv[hi, hi] = ui.astype(BF)
    linv[hi, lo] = (-dot32(li, keep[1])).astype(BF)
    uinv[lo, hi] = (-dot32(keep[0], ui)).astype(BF)
    linv[lo, hi] = jnp.zeros((HB, HB), BF)
    uinv[hi, lo] = jnp.zeros((HB, HB), BF)

MESH = pl.DeviceIdType.MESH
NCOL = 22
PER = 2
NCH = NCOL * PER
CH = NB // PER
NZ = 8
TICKS = 84
PACE = 4


def lag(d):
    return 5 * d


def comm(
    work, ring, q_out, patch, kept,
    rs, rr, ss, sr, kc, ksend, kloc, pr, pt, psend, ploc, loc, fs, fr,
    kb, pb, fb, pk1, pan, a, low, m, rows, cols, part,
):
    row = lax.axis_index("row")
    col = lax.axis_index("col")
    z, core = row // 2, row % 2
    x, y = col // 4, col % 4
    sib = row + 1 - 2 * core

    def pos(xx, yy):
        return ((xx + 4) % 4) * 4 + (yy + 4) % 4

    def rowof(zz, cc):
        return ((zz + NZ) % NZ) * 2 + cc

    def remote(src, dst, send, recv, dev):
        return pltpu.make_async_remote_copy(
            src_ref=src, dst_ref=dst, send_sem=send, recv_sem=recv, device_id=dev, device_id_type=MESH
        )

    barrier = pltpu.get_barrier_semaphore()

    def greet(dev):
        pl.semaphore_signal(barrier, inc=1, device_id=dev, device_id_type=MESH)

    greet((sib, col))

    near_root = (z == 1) | (z == NZ - 1)
    short = col < 2

    def one(cond, count):
        return jnp.where(cond, count, 0)

    @pl.when(core == 0)
    def _():
        greet((rowof(z + 1, 0), col))
        greet((rowof(z - 1, 0), col))
        for step in (1, -1):
            greet((row, pos(x, y + step)))
            greet((row, pos(x + step, y)))

        @pl.when((z == 0) & short)
        def _():
            greet((rowof(1, 1), col))
            greet((rowof(NZ - 1, 1), col))

        @pl.when(z == NZ - 1)
        def _():
            greet((rowof(0, 1), col))

        pl.semaphore_wait(barrier, 7 + one((z == 0) & short, 2) + one(z == NZ - 1, 1))

    @pl.when(core == 1)
    def _():
        @pl.when(short)
        def _():
            greet((rowof(z + 1, 1), col))
            greet((rowof(z - 1, 1), col))

            @pl.when(near_root)
            def _():
                greet((rowof(0, 0), col))

        @pl.when(x == 0)
        def _():
            for step in (1, 2, 3):
                greet((row, pos(x, y + step)))
                greet((row, pos(x + step, y)))

        @pl.when(x != 0)
        def _():
            greet((row, pos(0, y)))

        @pl.when(z == 0)
        def _():
            greet((rowof(NZ - 1, 0), col))

        pl.semaphore_wait(
            barrier,
            1 + one(z == 0, 1) + one(short, 2) + one(short & near_root, 1) + jnp.where(x == 0, 6, 1),
        )

    dist = [z, (NZ - z) % NZ]
    after = [rowof(z + 1, 0), rowof(z - 1, 0)]
    first = jnp.where(short, PER, 0)
    extra = jnp.where(short, 2, 0)

    def piece(ref, n):
        return ref.at[n // PER, pl.ds(pl.multiple_of((n % PER) * CH, CH), CH), :]

    def ahead(r, n, src):
        return remote(piece(src, n), piece(ring.at[r], n), rs.at[r, n], rr.at[r, n], (after[r], col))

    def across(r, n, src):
        return remote(piece(src, n), piece(ring.at[r], n), ss.at[r, n], sr.at[r, n], (sib, col))

    mine = work.at[0]
    fill = pltpu.make_async_copy(mine, ring.at[core], loc.at[0])
    keep = pltpu.make_async_copy(work, kept, loc.at[1])

    def loop(lo, hi, body):
        lax.fori_loop(lo, hi, lambda n, c: (body(n), c)[1], 0)

    def half(ref, h):
        return ref.at[pl.ds(h * HB, HB), :]

    def cuts(c, s):
        return range(2) if c == 0 and s == 0 else (None,)

    def cut(ref, h):
        return ref if h is None else half(ref, h)

    def kpiece(c, s, h):
        return cut(kb.at[c, s], h)

    def corner_sends(c, s):
        root = y == s
        up, down = (z > 0) & (z < 4), z > 5
        return [
            (root & ((up | (z == 0)) if c else up), (rowof(z + 1, 1), col)),
            (root & ((down | (z == 0)) if c else down), (rowof(z - 1, 1), col)),
            (root, (row, pos(x, y + 2))),
            (root, (row, pos(x, y + 1))),
            (root, (row, pos(x, y + 3))),
            (None, (row, pos(x + 2, y))),
            (None, (row, pos(x + 1, y))),
            (None, (row, pos(x + 3, y))),
        ]

    def each(c, s, act):
        @pl.when(x == 0)
        def _():
            for h in cuts(c, s):
                for slot, (cond, dev) in enumerate(corner_sends(c, s)):
                    copy = remote(
                        kpiece(c, s, h), kpiece(c, s, h), ksend.at[c, s, h or 0, slot], kc.at[c, s, h or 0], dev
                    )
                    if cond is None:
                        act(copy)
                    else:
                        pl.when(cond)(functools.partial(act, copy))

    def first_sends(s, act):
        for h in cuts(0, s):
            for slot, dev in enumerate(((rowof(1, 1), col), (rowof(NZ - 1, 1), col), (sib, col))):
                act(remote(
                    cut(mine.at[0], h), kpiece(0, s, h), ksend.at[0, s, h or 0, slot], kc.at[0, s, h or 0], dev
                ))

    def own_corner(s):
        return pltpu.make_async_copy(mine.at[0], kb.at[1, s], kloc.at[s])

    def corner_event(c, s):
        def arrive():
            for h in cuts(c, s):
                remote(
                    kpiece(c, s, h), kpiece(c, s, h), ksend.at[c, s, h or 0, 0], kc.at[c, s, h or 0], (row, col)
                ).wait_recv()

        if c == 0:
            arrive()
        else:
            here = (z == 0) & (x == 0) & (y == s)
            pl.when(here)(lambda: own_corner(s).wait())
            pl.when(jnp.logical_not(here))(arrive)
        each(c, s, lambda copy: copy.start())

    rel = [(y - s + 4) % 4 for s in range(2)]

    def is_root(s):
        return (x == 0) & (rel[s] == 0)

    def panel_sends(c, s):
        return [
            ((x == 0) & (rel[s] < 2), (row, pos(x, y + 1))),
            ((x == 0) & (rel[s] == 0), (row, pos(x, y - 1))),
            (x < 2, (row, pos(x + 1, y))),
            (x == 0, (row, pos(x - 1, y))),
        ]

    def each_panel(c, s, k, act):
        item = pb.at[c, s, k]
        for slot, (cond, dev) in enumerate(panel_sends(c, s)):
            pl.when(cond)(
                functools.partial(act, remote(item, item, psend.at[c, s, k, slot], pr.at[c, s, k], dev))
            )
        if c == 1:
            pl.when(jnp.logical_not(is_root(s)))(
                functools.partial(act, remote(item, item, psend.at[c, s, k, 4], pt.at[s, k], (sib, col)))
            )

    def own_panel(s, k):
        return pltpu.make_async_copy(work.at[k, 0], pb.at[core, s, k], ploc.at[s, k])

    def panel_event(c, s, k):
        item = pb.at[c, s, k]
        arrive = remote(item, item, psend.at[c, s, k, 0], pr.at[c, s, k], (row, col))
        if c == 0:
            @pl.when(is_root(s))
            def _():
                own_panel(s, k).wait()

            @pl.when(jnp.logical_not(is_root(s)))
            def _():
                arrive.wait_recv()
        else:
            arrive.wait_recv()
        each_panel(c, s, k, lambda copy: copy.start())

    def solve(s, k, block):
        out = dot16(block, fb[4 * s + 1]).astype(BF)
        pan[s, k] = jnp.where(k * 16 + row > s, out, jnp.zeros_like(out))

    def own_factors(c, recv):
        for k in range(2):
            solve(0, k, pb[c, 0, k])
        for k in range(2):
            block = (pb[c, 1, k].astype(F32) - dot16(pan[0, k], fb[3])).astype(BF)
            solve(1, k, block)
            left = dot16(pan[0, k], fb[0]) + dot16(pan[1, k], fb[6])
            right = dot16(pan[1, k], fb[4])
            if k == 0:
                left = jnp.where(row == c, -(fb[0] if c == 0 else fb[6]).astype(F32), left)
                right = jnp.where(row == c, jnp.zeros_like(right) if c == 0 else -fb[4].astype(F32), right)
            q_out[k, :, pl.ds(0, NB)] = left.astype(BF)
            q_out[k, :, pl.ds(NB, NB)] = right.astype(BF)
            if k == 0 and c == 0:
                patch[k] = jnp.where(
                    row == 0,
                    jnp.where(col == 0, fb[2], fb[3]),
                    jnp.where(col == 0, pan[0, k], pan[1, k]),
                )
            elif k == 0:
                patch[k] = jnp.where(
                    (row == 1) & (col != 0), pk1[...], jnp.where(col == 0, pan[0, k], pan[1, k])
                )
            else:
                patch[k] = jnp.where(col == 0, pan[0, k], pan[1, k])

    def give(i):
        return remote(fb.at[i], fb.at[i], fs.at[i], fr.at[i], (sib, col))

    @pl.when(core == 0)
    def _():
        for s in range(2):
            @pl.when(is_root(s) & (z == 0))
            def _():
                first_sends(s, lambda copy: copy.start())

        for s in range(2):
            @pl.when(is_root(s))
            def _():
                for k in range(2):
                    own_panel(s, k).start()

        @pl.when(z == 0)
        def _():
            fill.start()

        start = lag(jnp.minimum(z, NZ - z))

        solve_at = jnp.where((z == 1) | (z == NZ - 1), 72, TICKS - 1)

        def tick(t):
            @pl.when(t == 24)
            def _():
                keep.start()

            @pl.when(t == solve_at)
            def _():
                for i in range(7):
                    give(i).wait_recv()
                own_factors(0, None)

            for r in range(2):
                n = t - lag(dist[r]) - extra

                @pl.when((dist[r] > 0) & (n >= first) & (n < NCH))
                def _():
                    ahead(r, n, ring.at[r]).wait_recv()

                    @pl.when(dist[r] < NZ - 1)
                    def _():
                        ahead(r, n, ring.at[r]).start()

                    across(r, n, ring.at[r]).start()

            n = t - extra

            @pl.when((z == 0) & (n >= first) & (n < NCH))
            def _():
                ahead(0, n, mine).start()
                across(0, n, mine).start()

                @pl.when(n >= first + PACE)
                def _():
                    ahead(0, n - PACE, mine).wait_send()

            for s in range(2):
                hops = jnp.where(x == 0, 0, jnp.where(x == 2, 4, 3))
                hops = jnp.where(x == 0, jnp.where(rel[s] == 2, 2, jnp.minimum(rel[s], 1)), hops)
                for k in range(2):
                    for c in range(2):
                        @pl.when(t == start + 2 + 9 * hops + 2 * (4 * k + 2 * s + c))
                        def _():
                            panel_event(c, s, k)

        loop(0, TICKS, tick)
        keep.wait()

        for r in range(2):
            @pl.when((dist[r] > 0) & (dist[r] < NZ - 1))
            def _():
                loop(first, NCH, lambda n: ahead(r, n, mine).wait_send())

            @pl.when(dist[r] > 0)
            def _():
                loop(first, NCH, lambda n: across(r, n, mine).wait_send())

        @pl.when(z == 0)
        def _():
            fill.wait()
            loop(NCH - PACE, NCH, lambda n: ahead(0, n, mine).wait_send())
            loop(first, NCH, lambda n: across(0, n, mine).wait_send())
            loop(first, NCH, lambda n: across(1, n, mine).wait_recv())

        for s in range(2):
            @pl.when(is_root(s) & (z == 0))
            def _():
                first_sends(s, lambda copy: copy.wait_send())

        for c in range(2):
            for s in range(2):
                for k in range(2):
                    each_panel(c, s, k, lambda copy: copy.wait_send())

    @pl.when(core == 1)
    def _():
        def panel_give(s, k):
            return remote(work.at[k, 0], pb.at[1, s, k], psend.at[1, s, k, 0], pr.at[1, s, k], (sib, col))

        for s in range(2):
            @pl.when(is_root(s) & (z == 0))
            def _():
                own_corner(s).start()
                corner_event(1, s)

            @pl.when(is_root(s))
            def _():
                for k in range(2):
                    panel_give(s, k).start()
                    own_panel(s, k).start()

        @pl.when(z == 0)
        def _():
            fill.start()

            def both(n):
                ahead(1, n, mine).start()
                across(1, n, mine).start()

            loop(first, NCH, both)

        def others():
            for c, s in ((0, 1), (1, 0), (1, 1)):
                pl.when(jnp.logical_not(is_root(s)))(functools.partial(corner_event, c, s))

        pl.when(is_root(1))(functools.partial(corner_event, 0, 1))
        pl.when(is_root(1) & (z > 0))(functools.partial(corner_event, 1, 1))
        corner_event(0, 0)
        pl.when(is_root(0) & (z > 0))(functools.partial(corner_event, 1, 0))
        keep.start()
        a[...] = kb[0, 0].astype(F32)
        factor(a, fb.at[0], fb.at[1], fb.at[2], m, rows, cols, part, others)
        low[...] = dot16(kb[1, 0], fb[1]).astype(BF)
        fb[3] = dot16(fb[0], kb[0, 1]).astype(BF)
        for i in range(4):
            give(i).start()
        a[...] = (kb[1, 1].astype(F32) - dot16(low[...], fb[3])).astype(BF).astype(F32)
        factor(a, fb.at[4], fb.at[5], pk1, m, rows, cols, part)
        give(4).start()
        give(5).start()
        mid = dot16(low[...], fb[0]).astype(BF)
        fb[6] = (-dot16(fb[4], mid)).astype(BF)
        give(6).start()
        for s in range(2):
            for k in range(2):
                @pl.when(is_root(s))
                def _():
                    own_panel(s, k).wait()

                @pl.when(jnp.logical_not(is_root(s)))
                def _():
                    item = pb.at[1, s, k]
                    remote(item, item, psend.at[1, s, k, 4], pt.at[s, k], (sib, col)).wait_recv()
        own_factors(1, None)
        keep.wait()

        for i in range(7):
            give(i).wait_send()
        for s in range(2):
            for c in range(2):
                each(c, s, lambda copy: copy.wait_send())

            @pl.when(is_root(s))
            def _():
                for k in range(2):
                    panel_give(s, k).wait_send()

        loop(first, NCH, lambda n: across(0, n, mine).wait_recv())

        @pl.when(z == 0)
        def _():
            fill.wait()
            loop(first, NCH, lambda n: ahead(1, n, mine).wait_send())
            loop(first, NCH, lambda n: across(1, n, mine).wait_send())

        @pl.when(z > 0)
        def _():
            loop(first, NCH, lambda n: across(1, n, mine).wait_recv())


def gather(work):
    block = jax.ShapeDtypeStruct
    hbm = pl.BlockSpec(memory_space=pl.ANY)
    vm = pl.BlockSpec(memory_space=pltpu.VMEM)
    dma = pltpu.SemaphoreType.DMA
    mem = pltpu.VMEM
    return pl.pallas_call(
        comm,
        out_shape=(
            block((2, NCOL, NB, NB), BF),
            block((2, NB, 2 * NB), BF),
            block((2, NB, NB), BF),
            block((2, NCOL, NB, NB), BF),
        ),
        in_specs=[pl.BlockSpec(memory_space=pltpu.HBM)],
        out_specs=(hbm, vm, vm, vm),
        scratch_shapes=[
            dma((2, NCH)), dma((2, NCH)), dma((2, NCH)), dma((2, NCH)),
            dma((2, 2, 2)), dma((2, 2, 2, 8)), dma((2,)),
            dma((2, 2, 2)), dma((2, 2)), dma((2, 2, 2, 5)), dma((2, 2)),
            dma((2,)), dma((7,)), dma((7,)),
            mem((2, 2, NB, NB), BF),
            mem((2, 2, 2, NB, NB), BF),
            mem((7, NB, NB), BF),
            mem((NB, NB), BF),
            mem((2, 2, NB, NB), BF),
            mem((NB, NB), F32),
            mem((NB, NB), BF),
            mem((HB, HB), F32),
            mem((HB, HB), F32),
            mem((HB, HB), F32),
            mem((2, HB, HB), F32),
        ],
        compiler_params=pltpu.CompilerParams(
            collective_id=0, has_side_effects=True, vmem_limit_bytes=42 << 20
        ),
        name="gather",
    )(work)


def bulk(work, ring, q, patch, out, made, sem):
    row = lax.axis_index("row")
    col = lax.axis_index("col")

    def leave(k, j):
        return pltpu.make_async_copy(made.at[k, j], out.at[k, j], sem.at[k, j])

    def block(j):
        for k in range(2):
            change = dot16(q[k, :, :NB], ring[0, j]) + dot16(q[k, :, NB:], ring[1, j])
            base = work[k, j].astype(F32)
            if k == 0:
                base = base * factor_of_base
            made[k, j] = (base - change).astype(BF)

    factor_of_base = jnp.where(row < 2, 0.0, 1.0)
    block(0)

    @pl.when(col < 2)
    def _():
        for k in range(2):
            made[k, 0] = patch[k]

    for j in range(NCOL):
        if j:
            block(j)
        for k in range(2):
            leave(k, j).start()

    def settle(j, c):
        for k in range(2):
            leave(k, j).wait()
        return c

    lax.fori_loop(0, NCOL, settle, 0)


def update(work, ring, q, patch):
    vm = pl.BlockSpec(memory_space=pltpu.VMEM)
    return pl.pallas_call(
        bulk,
        out_shape=jax.ShapeDtypeStruct(work.shape, BF),
        in_specs=[vm] * 4,
        out_specs=pl.BlockSpec(memory_space=pltpu.HBM),
        scratch_shapes=[pltpu.VMEM(work.shape, BF), pltpu.SemaphoreType.DMA((2, NCOL))],
        compiler_params=pltpu.CompilerParams(vmem_limit_bytes=12 << 20),
        name="bulk",
    )(work, ring, q, patch)


def local(matrix):
    work = matrix.transpose(0, 1, 3, 4, 2, 5).reshape(2, NCOL, NB, NB)
    ring, q, patch, kept = gather(work)
    out = update(kept, ring, q, patch)
    return out.reshape(2, 1, NCOL, 1, NB, NB).transpose(0, 1, 4, 2, 3, 5)


def solution(mesh):
    spec = P(None, "row", None, None, "col", None)
    return jax.shard_map(local, mesh=mesh, in_specs=(spec,), out_specs=spec, check_vma=False)
```

```python
import functools

import jax
import jax.numpy as jnp
from jax import lax
from jax.experimental import pallas as pl
from jax.experimental.pallas import tpu as pltpu
from jax.sharding import PartitionSpec as P

NB = 256
HB = 128
BF = jnp.bfloat16
F32 = jnp.float32


def dot32(a, b):
    return jnp.dot(a, b, precision=lax.Precision.HIGHEST, preferred_element_type=F32)


def dot16(a, b):
    return jnp.dot(a, b, preferred_element_type=F32)


def pick_lane(x, lane):
    return jnp.take_along_axis(x, jnp.full(x.shape, lane, jnp.int32), axis=1)


def pick_row(x, row):
    return jnp.broadcast_to(x[row : row + 1, :], x.shape)


def eliminate(m, rows, cols):
    lane = lax.broadcasted_iota(jnp.int32, (8, HB), 1)
    sub = lax.broadcasted_iota(jnp.int32, (8, HB), 0)
    wide = lax.broadcasted_iota(jnp.int32, (HB, HB), 1)
    tall = lax.broadcasted_iota(jnp.int32, (HB, HB), 0)

    def group(g, carry):
        base = pl.multiple_of(g * 8, 8)
        own = m[pl.ds(base, 8), :]
        old = m[...]
        inside = (wide >= base) & (wide < base + 8)
        taken = jnp.where(inside, old, 0.0)
        hi = taken.astype(BF)
        lo = (taken - hi.astype(F32)).astype(BF)
        cb = [pick_lane(own, base + u) for u in range(8)]
        saved_row = jnp.zeros((8, HB), F32)
        saved_col = cols[pl.ds(base, 8), :]
        for t in range(8):
            here = lane == base + t
            at = sub == t
            inv = 1.0 / pick_row(cb[t], t)
            saved_row = jnp.where(at, own, saved_row)
            saved_col = jnp.where(here, jnp.where(at, inv, cb[t] * inv), saved_col)
            mult = jnp.where(at, -1.0, cb[t])
            scaled = jnp.where(here, 1.0, pick_row(own, t)) * inv
            own = jnp.where(here | at, 0.0, own) - mult * scaled
            for u in range(t + 1, 8):
                cb[u] = jnp.where(at, 0.0, cb[u]) - mult * (pick_row(cb[u], t) * inv)
        cols[...] = jnp.where(inside, old, cols[...])
        w = jnp.where((tall >= base) & (tall < base + 8), jnp.concatenate([own] * 16, 0), 0.0)
        wh = w.astype(BF)
        wl = (w - wh.astype(F32)).astype(BF)
        right = jnp.concatenate(
            [jnp.concatenate([wh, wl], 1), jnp.concatenate([wh, jnp.zeros_like(wl)], 1)], 0
        )
        both = dot16(jnp.concatenate([hi, lo], 1), right)
        m[...] = jnp.where(inside, 0.0, old) - (both[:, :HB] + both[:, HB:])
        m[pl.ds(base, 8), :] = own
        rows[pl.ds(base, 8), :] = saved_row
        cols[pl.ds(base, 8), :] = saved_col
        return carry

    lax.fori_loop(0, HB // 8, group, 0)


def pieces(m, rows, cols):
    i = lax.broadcasted_iota(jnp.int32, (HB, HB), 0)
    j = lax.broadcasted_iota(jnp.int32, (HB, HB), 1)
    near = (i // 8) == (j // 8)
    c = cols[...]
    r = rows[...]
    small = jnp.where(near & (i < j), -c, jnp.where(i == j, c, 0.0))
    far = dot32(jnp.where(near, 0.0, c), small)
    mixed = jnp.where(near, c, far)
    low = jnp.where(i > j, mixed, 0.0)
    upinv = jnp.where(i < j, -mixed, jnp.where(i == j, c, 0.0))
    lowinv = jnp.where(i > j, r, jnp.where(i == j, 1.0, 0.0))
    packed = jnp.where(i > j, low, r)
    return m[...], packed, lowinv, upinv


def factor(a, linv, uinv, packed, m, rows, cols, keep, between=None):
    lo, hi = pl.ds(0, HB), pl.ds(HB, HB)
    m[...] = a[lo, lo]
    eliminate(m, rows, cols)
    if between is not None:
        between()
    inv, pk, li, ui = pieces(m, rows, cols)
    a12, a21 = a[lo, hi], a[hi, lo]
    w = dot32(inv, a12)
    m[...] = a[hi, hi] - dot32(a21, w)
    keep[0] = w
    keep[1] = dot32(a21, inv)
    packed[lo, lo] = pk.astype(BF)
    packed[lo, hi] = dot32(li, a12).astype(BF)
    packed[hi, lo] = dot32(a21, ui).astype(BF)
    linv[lo, lo] = li.astype(BF)
    uinv[lo, lo] = ui.astype(BF)
    eliminate(m, rows, cols)
    inv, pk, li, ui = pieces(m, rows, cols)
    packed[hi, hi] = pk.astype(BF)
    linv[hi, hi] = li.astype(BF)
    uinv[hi, hi] = ui.astype(BF)
    linv[hi, lo] = (-dot32(li, keep[1])).astype(BF)
    uinv[lo, hi] = (-dot32(keep[0], ui)).astype(BF)
    linv[lo, hi] = jnp.zeros((HB, HB), BF)
    uinv[hi, lo] = jnp.zeros((HB, HB), BF)

MESH = pl.DeviceIdType.MESH
NCOL = 22
PER = 2
NCH = NCOL * PER
CH = NB // PER
NZ = 8
TICKS = 84
PACE = 4


def lag(d):
    return 5 * d


def comm(
    work, ring, q_out, patch, kept,
    rs, rr, ss, sr, kc, ksend, kloc, pr, pt, psend, ploc, loc, fs, fr,
    kb, pb, fb, pk1, pan, a, low, m, rows, cols, part,
):
    row = lax.axis_index("row")
    col = lax.axis_index("col")
    z, core = row // 2, row % 2
    x, y = col // 4, col % 4
    sib = row + 1 - 2 * core

    def pos(xx, yy):
        return ((xx + 4) % 4) * 4 + (yy + 4) % 4

    def rowof(zz, cc):
        return ((zz + NZ) % NZ) * 2 + cc

    def remote(src, dst, send, recv, dev):
        return pltpu.make_async_remote_copy(
            src_ref=src, dst_ref=dst, send_sem=send, recv_sem=recv, device_id=dev, device_id_type=MESH
        )

    barrier = pltpu.get_barrier_semaphore()

    def greet(dev):
        pl.semaphore_signal(barrier, inc=1, device_id=dev, device_id_type=MESH)

    greet((sib, col))

    near_root = (z == 1) | (z == NZ - 1)
    short = col < 2

    def one(cond, count):
        return jnp.where(cond, count, 0)

    @pl.when(core == 0)
    def _():
        greet((rowof(z + 1, 0), col))
        greet((rowof(z - 1, 0), col))
        for step in (1, -1):
            greet((row, pos(x, y + step)))
            greet((row, pos(x + step, y)))

        @pl.when((z == 0) & short)
        def _():
            greet((rowof(1, 1), col))
            greet((rowof(NZ - 1, 1), col))

        @pl.when(z == NZ - 1)
        def _():
            greet((rowof(0, 1), col))

        pl.semaphore_wait(barrier, 7 + one((z == 0) & short, 2) + one(z == NZ - 1, 1))

    @pl.when(core == 1)
    def _():
        @pl.when(short)
        def _():
            greet((rowof(z + 1, 1), col))
            greet((rowof(z - 1, 1), col))

            @pl.when(near_root)
            def _():
                greet((rowof(0, 0), col))

        @pl.when(x == 0)
        def _():
            for step in (1, 2, 3):
                greet((row, pos(x, y + step)))
                greet((row, pos(x + step, y)))

        @pl.when(x != 0)
        def _():
            greet((row, pos(0, y)))

        @pl.when(z == 0)
        def _():
            greet((rowof(NZ - 1, 0), col))

        pl.semaphore_wait(
            barrier,
            1 + one(z == 0, 1) + one(short, 2) + one(short & near_root, 1) + jnp.where(x == 0, 6, 1),
        )

    dist = [z, (NZ - z) % NZ]
    after = [rowof(z + 1, 0), rowof(z - 1, 0)]
    first = jnp.where(short, PER, 0)
    extra = 0

    def piece(ref, n):
        return ref.at[n // PER, pl.ds(pl.multiple_of((n % PER) * CH, CH), CH), :]

    def ahead(r, n, src):
        return remote(piece(src, n), piece(ring.at[r], n), rs.at[r, n], rr.at[r, n], (after[r], col))

    def across(r, n, src):
        return remote(piece(src, n), piece(ring.at[r], n), ss.at[r, n], sr.at[r, n], (sib, col))

    mine = work.at[0]
    fill = pltpu.make_async_copy(mine, ring.at[core], loc.at[0])
    keep = pltpu.make_async_copy(work, kept, loc.at[1])

    def loop(lo, hi, body):
        lax.fori_loop(lo, hi, lambda n, c: (body(n), c)[1], 0)

    def half(ref, h):
        return ref.at[pl.ds(h * HB, HB), :]

    def cuts(c, s):
        return range(2) if c == 0 and s == 0 else (None,)

    def cut(ref, h):
        return ref if h is None else half(ref, h)

    def kpiece(c, s, h):
        return cut(kb.at[c, s], h)

    def corner_sends(c, s):
        root = y == s
        up, down = (z > 0) & (z < 4), z > 5
        return [
            (root & ((up | (z == 0)) if c else up), (rowof(z + 1, 1), col)),
            (root & ((down | (z == 0)) if c else down), (rowof(z - 1, 1), col)),
            (root, (row, pos(x, y + 2))),
            (root, (row, pos(x, y + 1))),
            (root, (row, pos(x, y + 3))),
            (None, (row, pos(x + 2, y))),
            (None, (row, pos(x + 1, y))),
            (None, (row, pos(x + 3, y))),
        ]

    def each(c, s, act):
        @pl.when(x == 0)
        def _():
            for h in cuts(c, s):
                for slot, (cond, dev) in enumerate(corner_sends(c, s)):
                    copy = remote(
                        kpiece(c, s, h), kpiece(c, s, h), ksend.at[c, s, h or 0, slot], kc.at[c, s, h or 0], dev
                    )
                    if cond is None:
                        act(copy)
                    else:
                        pl.when(cond)(functools.partial(act, copy))

    def first_sends(s, act):
        for h in cuts(0, s):
            for slot, dev in enumerate(((rowof(1, 1), col), (rowof(NZ - 1, 1), col), (sib, col))):
                act(remote(
                    cut(mine.at[0], h), kpiece(0, s, h), ksend.at[0, s, h or 0, slot], kc.at[0, s, h or 0], dev
                ))

    def own_corner(s):
        return pltpu.make_async_copy(mine.at[0], kb.at[1, s], kloc.at[s])

    def corner_event(c, s):
        def arrive():
            for h in cuts(c, s):
                remote(
                    kpiece(c, s, h), kpiece(c, s, h), ksend.at[c, s, h or 0, 0], kc.at[c, s, h or 0], (row, col)
                ).wait_recv()

        if c == 0:
            arrive()
        else:
            here = (z == 0) & (x == 0) & (y == s)
            pl.when(here)(lambda: own_corner(s).wait())
            pl.when(jnp.logical_not(here))(arrive)
        each(c, s, lambda copy: copy.start())

    rel = [(y - s + 4) % 4 for s in range(2)]

    def is_root(s):
        return (x == 0) & (rel[s] == 0)

    def panel_sends(c, s):
        return [
            ((x == 0) & (rel[s] < 2), (row, pos(x, y + 1))),
            ((x == 0) & (rel[s] == 0), (row, pos(x, y - 1))),
            (x < 2, (row, pos(x + 1, y))),
            (x == 0, (row, pos(x - 1, y))),
        ]

    def each_panel(c, s, k, act):
        item = pb.at[c, s, k]
        for slot, (cond, dev) in enumerate(panel_sends(c, s)):
            pl.when(cond)(
                functools.partial(act, remote(item, item, psend.at[c, s, k, slot], pr.at[c, s, k], dev))
            )
        if c == 1:
            pl.when(jnp.logical_not(is_root(s)))(
                functools.partial(act, remote(item, item, psend.at[c, s, k, 4], pt.at[s, k], (sib, col)))
            )

    def own_panel(s, k):
        return pltpu.make_async_copy(work.at[k, 0], pb.at[core, s, k], ploc.at[s, k])

    def panel_event(c, s, k):
        item = pb.at[c, s, k]
        arrive = remote(item, item, psend.at[c, s, k, 0], pr.at[c, s, k], (row, col))
        if c == 0:
            @pl.when(is_root(s))
            def _():
                own_panel(s, k).wait()

            @pl.when(jnp.logical_not(is_root(s)))
            def _():
                arrive.wait_recv()
        else:
            arrive.wait_recv()
        each_panel(c, s, k, lambda copy: copy.start())

    def solve(s, k, block):
        out = dot16(block, fb[4 * s + 1]).astype(BF)
        pan[s, k] = jnp.where(k * 16 + row > s, out, jnp.zeros_like(out))

    def own_factors(c, recv):
        for k in range(2):
            solve(0, k, pb[c, 0, k])
        for k in range(2):
            block = (pb[c, 1, k].astype(F32) - dot16(pan[0, k], fb[3])).astype(BF)
            solve(1, k, block)
            left = dot16(pan[0, k], fb[0]) + dot16(pan[1, k], fb[6])
            right = dot16(pan[1, k], fb[4])
            if k == 0:
                left = jnp.where(row == c, -(fb[0] if c == 0 else fb[6]).astype(F32), left)
                right = jnp.where(row == c, jnp.zeros_like(right) if c == 0 else -fb[4].astype(F32), right)
            q_out[k, :, pl.ds(0, NB)] = left.astype(BF)
            q_out[k, :, pl.ds(NB, NB)] = right.astype(BF)
            if k == 0 and c == 0:
                patch[k] = jnp.where(
                    row == 0,
                    jnp.where(col == 0, fb[2], fb[3]),
                    jnp.where(col == 0, pan[0, k], pan[1, k]),
                )
            elif k == 0:
                patch[k] = jnp.where(
                    (row == 1) & (col != 0), pk1[...], jnp.where(col == 0, pan[0, k], pan[1, k])
                )
            else:
                patch[k] = jnp.where(col == 0, pan[0, k], pan[1, k])

    def give(i):
        return remote(fb.at[i], fb.at[i], fs.at[i], fr.at[i], (sib, col))

    @pl.when(core == 0)
    def _():
        for s in range(2):
            @pl.when(is_root(s) & (z == 0))
            def _():
                first_sends(s, lambda copy: copy.start())

        for s in range(2):
            @pl.when(is_root(s))
            def _():
                for k in range(2):
                    own_panel(s, k).start()

        @pl.when(z == 0)
        def _():
            fill.start()

        start = lag(jnp.minimum(z, NZ - z))

        solve_at = jnp.where((z == 1) | (z == NZ - 1), 72, TICKS - 1)

        def tick(t):
            @pl.when(t == 24)
            def _():
                keep.start()

            @pl.when(t == solve_at)
            def _():
                for i in range(7):
                    give(i).wait_recv()
                own_factors(0, None)

            for r in range(2):
                n = t - lag(dist[r]) - extra

                @pl.when((dist[r] > 0) & (n >= first) & (n < NCH))
                def _():
                    ahead(r, n, ring.at[r]).wait_recv()

                    @pl.when(dist[r] < NZ - 1)
                    def _():
                        ahead(r, n, ring.at[r]).start()

                    across(r, n, ring.at[r]).start()

            n = t - extra

            @pl.when((z == 0) & (n >= first) & (n < NCH))
            def _():
                ahead(0, n, mine).start()
                across(0, n, mine).start()

                @pl.when(n >= first + PACE)
                def _():
                    ahead(0, n - PACE, mine).wait_send()

            for s in range(2):
                hops = jnp.where(x == 0, 0, jnp.where(x == 2, 4, 3))
                hops = jnp.where(x == 0, jnp.where(rel[s] == 2, 2, jnp.minimum(rel[s], 1)), hops)
                for k in range(2):
                    for c in range(2):
                        @pl.when(t == start + 6 + 8 * hops + 2 * (4 * k + 2 * s + c))
                        def _():
                            panel_event(c, s, k)

        loop(0, TICKS, tick)
        keep.wait()

        for r in range(2):
            @pl.when((dist[r] > 0) & (dist[r] < NZ - 1))
            def _():
                loop(first, NCH, lambda n: ahead(r, n, mine).wait_send())

            @pl.when(dist[r] > 0)
            def _():
                loop(first, NCH, lambda n: across(r, n, mine).wait_send())

        @pl.when(z == 0)
        def _():
            fill.wait()
            loop(NCH - PACE, NCH, lambda n: ahead(0, n, mine).wait_send())
            loop(first, NCH, lambda n: across(0, n, mine).wait_send())
            loop(first, NCH, lambda n: across(1, n, mine).wait_recv())

        for s in range(2):
            @pl.when(is_root(s) & (z == 0))
            def _():
                first_sends(s, lambda copy: copy.wait_send())

        for c in range(2):
            for s in range(2):
                for k in range(2):
                    each_panel(c, s, k, lambda copy: copy.wait_send())

    @pl.when(core == 1)
    def _():
        def panel_give(s, k):
            return remote(work.at[k, 0], pb.at[1, s, k], psend.at[1, s, k, 0], pr.at[1, s, k], (sib, col))

        for s in range(2):
            @pl.when(is_root(s) & (z == 0))
            def _():
                own_corner(s).start()
                corner_event(1, s)

            @pl.when(is_root(s))
            def _():
                for k in range(2):
                    panel_give(s, k).start()
                    own_panel(s, k).start()

        @pl.when(z == 0)
        def _():
            fill.start()

            def both(n):
                ahead(1, n, mine).start()
                across(1, n, mine).start()

            loop(first, NCH, both)

        def others():
            for c, s in ((0, 1), (1, 0), (1, 1)):
                pl.when(jnp.logical_not(is_root(s)))(functools.partial(corner_event, c, s))

        pl.when(is_root(1))(functools.partial(corner_event, 0, 1))
        pl.when(is_root(1) & (z > 0))(functools.partial(corner_event, 1, 1))
        corner_event(0, 0)
        pl.when(is_root(0) & (z > 0))(functools.partial(corner_event, 1, 0))
        keep.start()
        a[...] = kb[0, 0].astype(F32)
        factor(a, fb.at[0], fb.at[1], fb.at[2], m, rows, cols, part, others)
        low[...] = dot16(kb[1, 0], fb[1]).astype(BF)
        fb[3] = dot16(fb[0], kb[0, 1]).astype(BF)
        for i in range(4):
            give(i).start()
        a[...] = (kb[1, 1].astype(F32) - dot16(low[...], fb[3])).astype(BF).astype(F32)
        factor(a, fb.at[4], fb.at[5], pk1, m, rows, cols, part)
        give(4).start()
        give(5).start()
        mid = dot16(low[...], fb[0]).astype(BF)
        fb[6] = (-dot16(fb[4], mid)).astype(BF)
        give(6).start()
        for s in range(2):
            for k in range(2):
                @pl.when(is_root(s))
                def _():
                    own_panel(s, k).wait()

                @pl.when(jnp.logical_not(is_root(s)))
                def _():
                    item = pb.at[1, s, k]
                    remote(item, item, psend.at[1, s, k, 4], pt.at[s, k], (sib, col)).wait_recv()
        own_factors(1, None)
        keep.wait()

        for i in range(7):
            give(i).wait_send()
        for s in range(2):
            for c in range(2):
                each(c, s, lambda copy: copy.wait_send())

            @pl.when(is_root(s))
            def _():
                for k in range(2):
                    panel_give(s, k).wait_send()

        loop(first, NCH, lambda n: across(0, n, mine).wait_recv())

        @pl.when(z == 0)
        def _():
            fill.wait()
            loop(first, NCH, lambda n: ahead(1, n, mine).wait_send())
            loop(first, NCH, lambda n: across(1, n, mine).wait_send())

        @pl.when(z > 0)
        def _():
            loop(first, NCH, lambda n: across(1, n, mine).wait_recv())


def gather(work):
    block = jax.ShapeDtypeStruct
    hbm = pl.BlockSpec(memory_space=pl.ANY)
    vm = pl.BlockSpec(memory_space=pltpu.VMEM)
    dma = pltpu.SemaphoreType.DMA
    mem = pltpu.VMEM
    return pl.pallas_call(
        comm,
        out_shape=(
            block((2, NCOL, NB, NB), BF),
            block((2, NB, 2 * NB), BF),
            block((2, NB, NB), BF),
            block((2, NCOL, NB, NB), BF),
        ),
        in_specs=[pl.BlockSpec(memory_space=pltpu.HBM)],
        out_specs=(hbm, vm, vm, vm),
        scratch_shapes=[
            dma((2, NCH)), dma((2, NCH)), dma((2, NCH)), dma((2, NCH)),
            dma((2, 2, 2)), dma((2, 2, 2, 8)), dma((2,)),
            dma((2, 2, 2)), dma((2, 2)), dma((2, 2, 2, 5)), dma((2, 2)),
            dma((2,)), dma((7,)), dma((7,)),
            mem((2, 2, NB, NB), BF),
            mem((2, 2, 2, NB, NB), BF),
            mem((7, NB, NB), BF),
            mem((NB, NB), BF),
            mem((2, 2, NB, NB), BF),
            mem((NB, NB), F32),
            mem((NB, NB), BF),
            mem((HB, HB), F32),
            mem((HB, HB), F32),
            mem((HB, HB), F32),
            mem((2, HB, HB), F32),
        ],
        compiler_params=pltpu.CompilerParams(
            collective_id=0, has_side_effects=True, vmem_limit_bytes=42 << 20
        ),
        name="gather",
    )(work)


def bulk(work, ring, q, patch, out, made, sem):
    row = lax.axis_index("row")
    col = lax.axis_index("col")

    def leave(k, j):
        return pltpu.make_async_copy(made.at[k, j], out.at[k, j], sem.at[k, j])

    def block(j):
        for k in range(2):
            change = dot16(q[k, :, :NB], ring[0, j]) + dot16(q[k, :, NB:], ring[1, j])
            base = work[k, j].astype(F32)
            if k == 0:
                base = base * factor_of_base
            made[k, j] = (base - change).astype(BF)

    factor_of_base = jnp.where(row < 2, 0.0, 1.0)
    block(0)

    @pl.when(col < 2)
    def _():
        for k in range(2):
            made[k, 0] = patch[k]

    for j in range(NCOL):
        if j:
            block(j)
        for k in range(2):
            leave(k, j).start()

    def settle(j, c):
        for k in range(2):
            leave(k, j).wait()
        return c

    lax.fori_loop(0, NCOL, settle, 0)


def update(work, ring, q, patch):
    vm = pl.BlockSpec(memory_space=pltpu.VMEM)
    return pl.pallas_call(
        bulk,
        out_shape=jax.ShapeDtypeStruct(work.shape, BF),
        in_specs=[vm] * 4,
        out_specs=pl.BlockSpec(memory_space=pltpu.HBM),
        scratch_shapes=[pltpu.VMEM(work.shape, BF), pltpu.SemaphoreType.DMA((2, NCOL))],
        compiler_params=pltpu.CompilerParams(vmem_limit_bytes=12 << 20),
        name="bulk",
    )(work, ring, q, patch)


def local(matrix):
    work = matrix.transpose(0, 1, 3, 4, 2, 5).reshape(2, NCOL, NB, NB)
    ring, q, patch, kept = gather(work)
    out = update(kept, ring, q, patch)
    return out.reshape(2, 1, NCOL, 1, NB, NB).transpose(0, 1, 4, 2, 3, 5)


def solution(mesh):
    spec = P(None, "row", None, None, "col", None)
    return jax.shard_map(local, mesh=mesh, in_specs=(spec,), out_specs=spec, check_vma=False)
```
